32 devices in a mesh: seg: 8 (over y, x, core), blk: 4 (over z).
Axes of the slice: x: 2, y: 2, z: 4, core: 2. Of those that a mesh axis runs over, the one named last changes fastest.
Arguments:
- spectra: bfloat16 [8, 4, 128, 4096], P('seg', 'blk'), may hold values from -6 to 6
- source_channels: int32 [4, 64], P('blk'), may hold values from 0 to 127, as said below
- pair_mask: int32 [4, 4], P('blk'), may hold values from 0 to 1, as said below
- channel_counts: int32 [4], P('blk'), may hold values from 64 to 128, as said below
Outputs:
- stacked: float32 [4, 4, 128, 1024], P('blk', None, 'seg')
The draws below stay inside these ranges and needn't reach their ends.
Inputs may be any that keep to these rules, and one draw needn't show every extreme that they name: `channel_counts`: every block has at least 64 live channels, and some block has all 128. `source_channels`: each block's 64 sources are distinct live channels of that block. `pair_mask`: slots whose offset leads past the fibre's ends are 0.
All inputs are finite; a program needn't handle non-finite values.
Results may differ from the reference program's by a relative error of at most 0.0095.
Values may be sent and summed in bfloat16 or wider, within the bound.
A program may use at most 64 MiB of HBM per device.

```python
import math
import jax
import jax.numpy as jnp
from jax import lax

CH = 128
BINS = 2048
LAGS = 16
SRC = 64
REACH = 2
NBLK = 4
SEGMENTS = 8


def block_draw(key):
    base = jax.random.fold_in(key, 7)
    key_count = jax.random.fold_in(base, 1)
    key_full = jax.random.fold_in(base, 2)
    key_rank = jax.random.fold_in(base, 3)
    block_ids = jnp.arange(NBLK, dtype=jnp.int32)
    live_counts = jax.random.randint(key_count, (NBLK,), CH // 2, CH + 1, dtype=jnp.int32)
    full_block = jax.random.randint(key_full, (), 0, NBLK, dtype=jnp.int32)
    live_counts = jnp.where(block_ids == full_block, CH, live_counts)
    channel_ids = jnp.arange(CH, dtype=jnp.int32)
    priority = jax.random.randint(key_rank, (NBLK, CH), 0, 1024, dtype=jnp.int32) * CH + channel_ids[None, :]
    priority = jnp.where(channel_ids[None, :] < live_counts[:, None], priority, priority + 2048 * CH)
    ranking = jnp.argsort(priority, axis=1)
    return (live_counts.astype(jnp.int32), ranking[:, :SRC].astype(jnp.int32))


def draw_channel_counts(key, part):
    return block_draw(key)[0]


def draw_source_channels(key, part):
    return block_draw(key)[1]


def draw_pair_mask(key, part):
    coin_flips = jax.random.randint(jax.random.fold_in(key, 11), (NBLK, 2 * REACH), 0, 4, dtype=jnp.int32)
    slot_ids = jnp.arange(2 * REACH, dtype=jnp.int32)
    offsets = jnp.where(slot_ids < REACH, slot_ids - REACH, slot_ids - REACH + 1)
    target = jnp.arange(NBLK, dtype=jnp.int32)[:, None] + offsets[None, :]
    inside = jnp.logical_and(target >= 0, target < NBLK)
    return jnp.where(jnp.logical_and(coin_flips > 0, inside), 1, 0).astype(jnp.int32)


def levels(stream_key, shape, pieces, low, top_value):
    def one(position, blocks):
        steps = jax.random.uniform(jax.random.fold_in(jax.random.fold_in(stream_key, 6), position), (blocks,), jnp.float32, low / len(pieces), top_value / len(pieces))
        return jnp.repeat(jnp.exp(steps), shape[position] // blocks).reshape((-1,) + (1,) * (len(shape) - position - 1))

    factor_of = one(*pieces[0])
    for cut in pieces[1:]:
        factor_of = factor_of * one(*cut)
    return factor_of


def gaussian(own_key, shape, spread, most, shards=(), held_as=jnp.bfloat16):
    result = spread * jax.random.normal(own_key, shape, jnp.float32)
    if shards:
        result = result * levels(own_key, shape, shards, -0.22, 0.18)
    return jnp.clip(result, -most, most).astype(held_as)


def setup_inputs(seed: int = 0) -> dict:
    seeds = jax.random.split(jax.random.key(seed), 5)
    spectra = gaussian(seeds[0], (SEGMENTS, NBLK, CH, 2 * BINS), 1.0, 6.0, ((0, 8), (1, 4)))
    source_channels = draw_source_channels(jax.random.fold_in(seeds[4], 71), 0)
    pair_mask = draw_pair_mask(jax.random.fold_in(seeds[4], 71), 0)
    channel_counts = draw_channel_counts(jax.random.fold_in(seeds[4], 71), 0)
    return dict(spectra=spectra, source_channels=source_channels, pair_mask=pair_mask, channel_counts=channel_counts)


def slot_offsets():
    return [slot_index - REACH if slot_index < REACH else slot_index - REACH + 1 for slot_index in range(2 * REACH)]

def make_table(bin_count, lag_count):
    freq_index = lax.broadcasted_iota(jnp.int32, (bin_count, lag_count), 0)
    lag_index = lax.broadcasted_iota(jnp.int32, (bin_count, lag_count), 1) - lag_count // 2
    turn_count = jnp.mod(freq_index * lag_index, 2 * bin_count)
    phase_angle = turn_count.astype(jnp.float32) * (math.pi / bin_count)
    scaling = 1.0 / math.sqrt(2.0 * bin_count)
    return jnp.concatenate([jnp.cos(phase_angle) * scaling, -jnp.sin(phase_angle) * scaling], axis=0).astype(jnp.bfloat16)

def source_kernel(sources, table):
    bin_count = table.shape[0] // 2
    source_re = sources[:, :bin_count].astype(jnp.float32).T[:, :, None]
    source_im = sources[:, bin_count:].astype(jnp.float32).T[:, :, None]
    table_re = table[:bin_count].astype(jnp.float32)[:, None, :]
    table_im = table[bin_count:].astype(jnp.float32)[:, None, :]
    upper = source_re * table_re + source_im * table_im
    lower = source_im * table_re - source_re * table_im
    joined = jnp.concatenate([upper, lower], axis=0)
    return joined.reshape(2 * bin_count, -1).astype(jnp.bfloat16)

def reference(spectra, source_channels, pair_mask, channel_counts):
    lag_table = make_table(BINS, LAGS)
    channel_ids = jnp.arange(CH, dtype=jnp.int32)
    live_rows = channel_ids[None, :] < channel_counts[:, None]
    masked = jnp.where(live_rows[None, :, :, None], spectra, jnp.zeros_like(spectra))
    offsets = slot_offsets()

    def per_block(block_index):
        own_block = lax.dynamic_index_in_dim(masked, block_index, 1, keepdims=False)
        chosen = lax.dynamic_index_in_dim(source_channels, block_index, 0, keepdims=False)
        flags = lax.dynamic_index_in_dim(pair_mask, block_index, 0, keepdims=False)
        weights = []
        neighbours = []
        for slot_index, offset in enumerate(offsets):
            target = block_index + offset
            inside = jnp.logical_and(target >= 0, target < NBLK)
            neighbours.append(lax.dynamic_index_in_dim(masked, jnp.clip(target, 0, NBLK - 1).astype(jnp.int32), 1, keepdims=False))
            weights.append(jnp.where(inside, flags[slot_index], 0).astype(jnp.float32))

        def add_segment(segment, running):
            sources = jnp.take(own_block[segment], chosen, axis=0)
            kernel = source_kernel(sources, lag_table)
            terms = [jnp.dot(near[segment], kernel, preferred_element_type=jnp.float32) * weight for near, weight in zip(neighbours, weights)]
            return running + jnp.stack(terms)
        return lax.fori_loop(0, SEGMENTS, add_segment, jnp.zeros((2 * REACH, CH, SRC * LAGS), jnp.float32))
    stacked = lax.map(per_block, jnp.arange(NBLK, dtype=jnp.int32))
    return stacked * (1.0 / math.sqrt(SEGMENTS))
```

```python
import functools
import math

import ml_dtypes
import numpy as np

import jax
import jax.numpy as jnp
from jax import lax
from jax.experimental import pallas as pl
from jax.experimental.pallas import tpu as pltpu
from jax.sharding import PartitionSpec as P

LAGS = 16
REACH = 2
GROUPS = 2
CHUNK = 512
MESH = pl.DeviceIdType.MESH


def make_table(bin_count, lag_count):
    lag_index = np.arange(lag_count)[:, None] - lag_count // 2
    turn_count = np.mod(np.arange(bin_count)[None, :] * lag_index, 2 * bin_count)
    phase_angle = turn_count.astype(np.float32) * np.float32(math.pi / bin_count)
    scaling = np.float32(1.0 / math.sqrt(2.0 * bin_count))
    both = np.stack([np.cos(phase_angle) * scaling, -np.sin(phase_angle) * scaling])
    return both.astype(ml_dtypes.bfloat16).astype(np.float32)


def body(n, nz, spectra, table, chosen, count, out, own, src, kbuf_a, kbuf_b, acc,
         part, landed, back, own_send, fwd_send, src_recv, part_send, part_recv,
         back_send, back_recv):
    k = lax.axis_index("seg")
    m = lax.axis_index("blk")
    channels, width = spectra.shape
    bins = width // 2
    rows = channels // n
    group = own.shape[1]
    cols = group * LAGS

    barrier = pltpu.get_barrier_semaphore()

    @pl.loop(1, n)
    def _(rel):
        pl.semaphore_signal(barrier, inc=1, device_id={"seg": lax.rem(k + rel, n)},
                            device_id_type=MESH)

    def along(dz):
        return jnp.logical_and(m + dz >= 0, m + dz < nz)

    for dz in (-2, -1, 1, 2):
        @pl.when(along(dz))
        def _():
            pl.semaphore_signal(barrier, inc=1, device_id={"blk": m + dz}, device_id_type=MESH)

    lane = lax.broadcasted_iota(jnp.int32, (GROUPS * group, channels), 1)
    hit = jnp.logical_and(lane == chosen[...], lane < count[0])
    one_hot = jnp.where(hit, 1.0, 0.0).astype(jnp.bfloat16)
    for c in range(width // CHUNK):
        at = pl.ds(c * CHUNK, CHUNK)
        picked = jnp.dot(one_hot, spectra[:, at], preferred_element_type=jnp.float32)
        picked = picked.astype(jnp.bfloat16)
        for g in range(GROUPS):
            own[g, :, at] = picked[g * group:(g + 1) * group]
    live = lax.broadcasted_iota(jnp.int32, (channels, 1), 0) < count[0]
    live = jnp.where(live, 1.0, 0.0)

    near = jnp.minimum(m, REACH) + jnp.minimum(nz - 1 - m, REACH)
    pl.semaphore_wait(barrier, n - 1 + near)

    def slot_of(side, dist):
        return 1 + dist if side == 0 else 2 - dist

    def step(side):
        return 1 if side == 0 else -1

    def own_copy(side, g):
        return pltpu.make_async_remote_copy(
            own.at[g], src.at[slot_of(side, 1), g], own_send.at[side, g],
            src_recv.at[slot_of(side, 1), g], device_id={"blk": m + step(side)},
            device_id_type=MESH)

    def fwd_copy(side, g):
        return pltpu.make_async_remote_copy(
            src.at[slot_of(side, 1), g], src.at[slot_of(side, 2), g], fwd_send.at[side, g],
            src_recv.at[slot_of(side, 2), g], device_id={"blk": m + step(side)},
            device_id_type=MESH)

    def part_copy(slot, g, peer, sender):
        return pltpu.make_async_remote_copy(
            part.at[slot, g, peer], landed.at[slot, g, sender], part_send.at[slot, g, peer],
            part_recv.at[slot, g, sender], device_id={"seg": peer}, device_id_type=MESH)

    def back_copy(slot, g, owner):
        at = pl.ds(pl.multiple_of(g * cols, cols), cols)
        return pltpu.make_async_remote_copy(
            back.at[slot, g], out.at[slot, :, at], back_send.at[slot, g],
            back_recv.at[slot, g], device_id={"blk": owner}, device_id_type=MESH)

    def has(side, dist):
        return m >= dist if side == 0 else m + dist < nz

    for g in range(GROUPS):
        for side in range(2):
            @pl.when(along(step(side)))
            def _():
                own_copy(side, g).start()

    def expand(slot, g, first, kbuf):
        re_at, im_at = pl.ds(first, CHUNK), pl.ds(bins + first, CHUNK)
        t_re, t_im = table[0, :, re_at], table[1, :, re_at]
        s_re = src[slot, g, :, re_at].astype(jnp.float32)
        s_im = src[slot, g, :, im_at].astype(jnp.float32)
        for j in range(group):
            a, b = s_re[j:j + 1], s_im[j:j + 1]
            to = slice(j * LAGS, (j + 1) * LAGS)
            kbuf[to, :CHUNK] = (a * t_re + b * t_im).astype(jnp.bfloat16)
            kbuf[to, CHUNK:] = (b * t_re - a * t_im).astype(jnp.bfloat16)

    def contract(first, kbuf):
        dims = (((1,), (1,)), ((), ()))
        got = lax.dot_general(kbuf[:, :CHUNK], spectra[:, pl.ds(first, CHUNK)], dims,
                              preferred_element_type=jnp.float32)
        return got + lax.dot_general(kbuf[:, CHUNK:], spectra[:, pl.ds(bins + first, CHUNK)],
                                     dims, preferred_element_type=jnp.float32)

    def correlate(slot, g):
        acc[...] = jnp.zeros_like(acc)

        @pl.loop(0, bins // (2 * CHUNK))
        def _(i):
            first = pl.multiple_of(i * 2 * CHUNK, CHUNK)
            second = pl.multiple_of(first + CHUNK, CHUNK)
            expand(slot, g, first, kbuf_a)
            got = contract(first, kbuf_a)
            expand(slot, g, second, kbuf_b)
            acc[...] += got + contract(second, kbuf_b)

        turned = acc[...].T * live
        for q in range(n):
            part[slot, g, q] = turned[q * rows:(q + 1) * rows].astype(jnp.bfloat16)

        @pl.loop(1, n)
        def _(rel):
            part_copy(slot, g, lax.rem(k + rel, n), k).start()

    def finish(p):
        dist, g = p // GROUPS + 1, p % GROUPS
        for side in range(2):
            slot = slot_of(side, dist)

            @pl.when(has(side, dist))
            def _():
                total = part[slot, g, k].astype(jnp.float32)
                for rel in range(1, n):
                    sender = lax.rem(k + rel, n)
                    part_copy(slot, g, sender, sender).wait_recv()
                    total = total + landed[slot, g, sender].astype(jnp.float32)
                back[slot, g] = total.astype(jnp.bfloat16)
                back_copy(slot, g, m - dist * step(side)).start()

    @pl.loop(0, REACH * GROUPS)
    def _(p):
        dist, g = p // GROUPS + 1, p % GROUPS
        for side in range(2):
            @pl.when(has(side, dist))
            def _():
                slot = slot_of(side, dist)
                pltpu.make_async_copy(src.at[slot, g], src.at[slot, g],
                                      src_recv.at[slot, g]).wait()

                @pl.when(jnp.logical_and(dist == 1, along(step(side))))
                def _():
                    fwd_copy(side, g).start()

        for side in range(2):
            @pl.when(has(side, dist))
            def _():
                correlate(slot_of(side, dist), g)

        @pl.when(p > 0)
        def _():
            finish(p - 1)

    finish(REACH * GROUPS - 1)

    for slot in range(2 * REACH):
        offset = slot - REACH if slot < REACH else slot - REACH + 1

        @pl.when(jnp.logical_not(along(offset)))
        def _():
            out[slot] = jnp.zeros(out.shape[1:], out.dtype)

        @pl.when(along(offset))
        def _():
            for g in range(GROUPS):
                back_copy(slot, g, m + offset).wait_recv()

    for g in range(GROUPS):
        for side in range(2):
            @pl.when(along(step(side)))
            def _():
                own_copy(side, g).wait_send()

            @pl.when(jnp.logical_and(has(side, 1), along(step(side))))
            def _():
                fwd_copy(side, g).wait_send()

            for dist in range(1, REACH + 1):
                @pl.when(has(side, dist))
                def _():
                    slot = slot_of(side, dist)
                    back_copy(slot, g, m - dist * step(side)).wait_send()

                    @pl.loop(1, n)
                    def _(rel):
                        part_copy(slot, g, lax.rem(k + rel, n), k).wait_send()


def local(n, nz, spectra, source_channels, pair_mask, channel_counts):
    own_block = spectra[0, 0]
    channels, width = own_block.shape
    sources = source_channels.shape[1]
    group = sources // GROUPS
    rows, cols, slots = channels // n, group * LAGS, 2 * REACH
    table = jnp.asarray(make_table(width // 2, LAGS))
    vmem = pl.BlockSpec(memory_space=pltpu.VMEM)
    dma = pltpu.SemaphoreType.DMA
    flops = 2 * slots * channels * width * sources * LAGS
    got = pl.pallas_call(
        functools.partial(body, n, nz),
        out_shape=jax.ShapeDtypeStruct((slots, rows, sources * LAGS), jnp.bfloat16),
        in_specs=[vmem, vmem, vmem, pl.BlockSpec(memory_space=pltpu.SMEM)],
        out_specs=vmem,
        scratch_shapes=[
            pltpu.VMEM((GROUPS, group, width), jnp.bfloat16),
            pltpu.VMEM((slots, GROUPS, group, width), jnp.bfloat16),
            pltpu.VMEM((cols, 2 * CHUNK), jnp.bfloat16),
            pltpu.VMEM((cols, 2 * CHUNK), jnp.bfloat16),
            pltpu.VMEM((cols, channels), jnp.float32),
            pltpu.VMEM((slots, GROUPS, n, rows, cols), jnp.bfloat16),
            pltpu.VMEM((slots, GROUPS, n, rows, cols), jnp.bfloat16),
            pltpu.VMEM((slots, GROUPS, rows, cols), jnp.bfloat16),
            dma((2, GROUPS)),
            dma((2, GROUPS)),
            dma((slots, GROUPS)),
            dma((slots, GROUPS, n)),
            dma((slots, GROUPS, n)),
            dma((slots, GROUPS)),
            dma((slots, GROUPS)),
        ],
        compiler_params=pltpu.CompilerParams(
            collective_id=0, has_side_effects=True, vmem_limit_bytes=40 * 2**20),
        cost_estimate=pl.CostEstimate(flops=flops, bytes_accessed=2 * channels * width,
                                      transcendentals=0),
    )(own_block, table, source_channels.reshape(sources, 1), channel_counts)
    weights = pair_mask[0].astype(jnp.float32) * (1.0 / math.sqrt(n))
    return (got.astype(jnp.float32) * weights[:, None, None])[None]


def solution(mesh):
    in_specs = (P("seg", "blk", None, None), P("blk", None), P("blk", None), P("blk"))
    out_specs = P("blk", None, "seg", None)
    part = functools.partial(local, mesh.shape["seg"], mesh.shape["blk"])
    return jax.shard_map(part, mesh=mesh, in_specs=in_specs, out_specs=out_specs, check_vma=False)
```

```python
import functools
import math

import ml_dtypes
import numpy as np

import jax
import jax.numpy as jnp
from jax import lax
from jax.experimental import pallas as pl
from jax.experimental.pallas import tpu as pltpu
from jax.sharding import PartitionSpec as P

LAGS = 16
REACH = 2
GROUPS = 2
PIECES = 4
PICK = 512
MESH = pl.DeviceIdType.MESH


def make_table(bin_count, lag_count):
    lag_index = np.arange(lag_count)[:, None] - lag_count // 2
    turn_count = np.mod(np.arange(bin_count)[None, :] * lag_index, 2 * bin_count)
    phase_angle = turn_count.astype(np.float32) * np.float32(math.pi / bin_count)
    scaling = np.float32(1.0 / math.sqrt(2.0 * bin_count))
    both = np.stack([np.cos(phase_angle) * scaling, -np.sin(phase_angle) * scaling])
    return both.astype(ml_dtypes.bfloat16)


def body(n, nz, spectra_in, table_in, chosen_in, count_in, out, spectra, table, chosen, count,
         own, src, kbuf_a, kbuf_b, acc, part, landed, back, in_sem, own_send, fwd_send, src_recv,
         part_send, part_recv, back_send, back_recv):
    arrivals = [
        pltpu.make_async_copy(here, there, in_sem.at[i])
        for i, (here, there) in enumerate([(chosen_in, chosen), (count_in, count),
                                           (spectra_in, spectra), (table_in, table)])
    ]
    for arrival in arrivals:
        arrival.start()

    k = lax.axis_index("seg")
    m = lax.axis_index("blk")
    channels, width = spectra.shape
    bins = width // 2
    rows = channels // n
    group = own.shape[2]
    cols = group * LAGS
    span = bins // PIECES
    chunk = span // 2

    barrier = pltpu.get_barrier_semaphore()

    @pl.loop(1, n)
    def _(rel):
        pl.semaphore_signal(barrier, inc=1, device_id={"seg": lax.rem(k + rel, n)},
                            device_id_type=MESH)

    def along(dz):
        return jnp.logical_and(m + dz >= 0, m + dz < nz)

    for dz in (-2, -1, 1, 2):
        @pl.when(along(dz))
        def _():
            pl.semaphore_signal(barrier, inc=1, device_id={"blk": m + dz}, device_id_type=MESH)

    for arrival in arrivals:
        arrival.wait()

    channel = lax.broadcasted_iota(jnp.int32, (channels, GROUPS * group), 0)
    hit = jnp.logical_and(channel == chosen[...], channel < count[0])
    one_hot = jnp.where(hit, 1.0, 0.0).T.astype(jnp.bfloat16)
    for i in range(PIECES):
        for half in range(2):
            for c in range(0, span, PICK):
                picked = jnp.dot(one_hot, spectra[:, pl.ds(half * bins + i * span + c, PICK)],
                                 preferred_element_type=jnp.float32).astype(jnp.bfloat16)
                for g in range(GROUPS):
                    own[g, i, :, pl.ds(half * span + c, PICK)] = picked[g * group:(g + 1) * group]
    live = lax.broadcasted_iota(jnp.int32, (channels, 1), 0) < count[0]
    live = jnp.where(live, 1.0, 0.0)

    near = jnp.minimum(m, REACH) + jnp.minimum(nz - 1 - m, REACH)
    pl.semaphore_wait(barrier, n - 1 + near)

    def slot_of(side, dist):
        return 1 + dist if side == 0 else 2 - dist

    def step(side):
        return 1 if side == 0 else -1

    def own_copy(side, g, i):
        return pltpu.make_async_remote_copy(
            own.at[g, i], src.at[slot_of(side, 1), g, i], own_send.at[side, g, i],
            src_recv.at[slot_of(side, 1), g, i], device_id={"blk": m + step(side)},
            device_id_type=MESH)

    def fwd_copy(side, g, i):
        return pltpu.make_async_remote_copy(
            src.at[slot_of(side, 1), g, i], src.at[slot_of(side, 2), g, i],
            fwd_send.at[side, g, i], src_recv.at[slot_of(side, 2), g, i],
            device_id={"blk": m + step(side)}, device_id_type=MESH)

    def src_wait(slot, g, i):
        here = src.at[slot, g, i]
        pltpu.make_async_copy(here, here, src_recv.at[slot, g, i]).wait()

    def part_copy(slot, g, peer, sender):
        return pltpu.make_async_remote_copy(
            part.at[slot, g, peer], landed.at[slot, g, sender], part_send.at[slot, g, peer],
            part_recv.at[slot, g, sender], device_id={"seg": peer}, device_id_type=MESH)

    def back_copy(slot, g, owner):
        at = pl.ds(pl.multiple_of(g * cols, cols), cols)
        return pltpu.make_async_remote_copy(
            back.at[slot, g], out.at[slot, :, at], back_send.at[slot, g],
            back_recv.at[slot, g], device_id={"blk": owner}, device_id_type=MESH)

    def has(side, dist):
        return m >= dist if side == 0 else m + dist < nz

    for g in range(GROUPS):
        for side in range(2):
            @pl.when(along(step(side)))
            def _():
                for i in range(PIECES):
                    own_copy(side, g, i).start()

    def expand(slot, g, i, part_of, kbuf):
        at = pl.ds(pl.multiple_of(i * span + part_of * chunk, chunk), chunk)
        t_re, t_im = table[0, :, at], table[1, :, at]
        s_re = src[slot, g, i, :, pl.ds(part_of * chunk, chunk)]
        s_im = src[slot, g, i, :, pl.ds(span + part_of * chunk, chunk)]
        for j in range(group):
            a, b = s_re[j:j + 1], s_im[j:j + 1]
            to = slice(j * LAGS, (j + 1) * LAGS)
            kbuf[to, :chunk] = a * t_re + b * t_im
            kbuf[to, chunk:] = b * t_re - a * t_im

    def contract(i, part_of, kbuf):
        dims = (((1,), (1,)), ((), ()))
        first = pl.multiple_of(i * span + part_of * chunk, chunk)
        got = lax.dot_general(kbuf[:, :chunk], spectra[:, pl.ds(first, chunk)], dims,
                              preferred_element_type=jnp.float32)
        return got + lax.dot_general(kbuf[:, chunk:], spectra[:, pl.ds(bins + first, chunk)],
                                     dims, preferred_element_type=jnp.float32)

    def correlate(slot, dist, g):
        acc[...] = jnp.zeros_like(acc)

        @pl.loop(0, PIECES)
        def _(i):
            @pl.when(dist > 1)
            def _():
                src_wait(slot, g, i)

            expand(slot, g, i, 0, kbuf_a)
            got = contract(i, 0, kbuf_a)
            expand(slot, g, i, 1, kbuf_b)
            acc[...] += got + contract(i, 1, kbuf_b)

        turned = acc[...].T * live
        for q in range(n):
            part[slot, g, q] = turned[q * rows:(q + 1) * rows].astype(jnp.bfloat16)

        @pl.loop(1, n)
        def _(rel):
            part_copy(slot, g, lax.rem(k + rel, n), k).start()

    def finish(p):
        dist, g = p // GROUPS + 1, p % GROUPS
        for side in range(2):
            slot = slot_of(side, dist)

            @pl.when(has(side, dist))
            def _():
                total = part[slot, g, k].astype(jnp.float32)
                for rel in range(1, n):
                    sender = lax.rem(k + rel, n)
                    part_copy(slot, g, sender, sender).wait_recv()
                    total = total + landed[slot, g, sender].astype(jnp.float32)
                back[slot, g] = total.astype(jnp.bfloat16)
                back_copy(slot, g, m - dist * step(side)).start()

    @pl.loop(0, REACH * GROUPS)
    def _(p):
        dist, g = p // GROUPS + 1, p % GROUPS
        for side in range(2):
            for i in range(PIECES):
                @pl.when(jnp.logical_and(dist == 1, has(side, 1)))
                def _():
                    src_wait(slot_of(side, 1), g, i)

                    @pl.when(along(step(side)))
                    def _():
                        fwd_copy(side, g, i).start()

        for side in range(2):
            @pl.when(has(side, dist))
            def _():
                correlate(slot_of(side, dist), dist, g)

        @pl.when(p > 0)
        def _():
            finish(p - 1)

    finish(REACH * GROUPS - 1)

    for slot in range(2 * REACH):
        offset = slot - REACH if slot < REACH else slot - REACH + 1

        @pl.when(jnp.logical_not(along(offset)))
        def _():
            out[slot] = jnp.zeros(out.shape[1:], out.dtype)

        @pl.when(along(offset))
        def _():
            for g in range(GROUPS):
                back_copy(slot, g, m + offset).wait_recv()

    for g in range(GROUPS):
        for side in range(2):
            @pl.when(along(step(side)))
            def _():
                for i in range(PIECES):
                    own_copy(side, g, i).wait_send()

            @pl.when(jnp.logical_and(has(side, 1), along(step(side))))
            def _():
                for i in range(PIECES):
                    fwd_copy(side, g, i).wait_send()

            for dist in range(1, REACH + 1):
                @pl.when(has(side, dist))
                def _():
                    slot = slot_of(side, dist)
                    back_copy(slot, g, m - dist * step(side)).wait_send()

                    @pl.loop(1, n)
                    def _(rel):
                        part_copy(slot, g, lax.rem(k + rel, n), k).wait_send()


def local(n, nz, spectra, source_channels, pair_mask, channel_counts):
    own_block = spectra[0, 0]
    channels, width = own_block.shape
    sources = source_channels.shape[1]
    group = sources // GROUPS
    rows, cols, slots = channels // n, group * LAGS, 2 * REACH
    table = jnp.asarray(make_table(width // 2, LAGS))
    vmem = pl.BlockSpec(memory_space=pltpu.VMEM)
    dma = pltpu.SemaphoreType.DMA
    flops = 2 * slots * channels * width * sources * LAGS
    got = pl.pallas_call(
        functools.partial(body, n, nz),
        out_shape=jax.ShapeDtypeStruct((slots, rows, sources * LAGS), jnp.bfloat16),
        in_specs=[pl.BlockSpec(memory_space=pl.ANY)] * 4,
        out_specs=vmem,
        scratch_shapes=[
            pltpu.VMEM(own_block.shape, jnp.bfloat16),
            pltpu.VMEM(table.shape, jnp.bfloat16),
            pltpu.VMEM((1, sources), jnp.int32),
            pltpu.SMEM((1,), jnp.int32),
            pltpu.VMEM((GROUPS, PIECES, group, width // PIECES), jnp.bfloat16),
            pltpu.VMEM((slots, GROUPS, PIECES, group, width // PIECES), jnp.bfloat16),
            pltpu.VMEM((cols, width // PIECES // 2), jnp.bfloat16),
            pltpu.VMEM((cols, width // PIECES // 2), jnp.bfloat16),
            pltpu.VMEM((cols, channels), jnp.float32),
            pltpu.VMEM((slots, GROUPS, n, rows, cols), jnp.bfloat16),
            pltpu.VMEM((slots, GROUPS, n, rows, cols), jnp.bfloat16),
            pltpu.VMEM((slots, GROUPS, rows, cols), jnp.bfloat16),
            dma((4,)),
            dma((2, GROUPS, PIECES)),
            dma((2, GROUPS, PIECES)),
            dma((slots, GROUPS, PIECES)),
            dma((slots, GROUPS, n)),
            dma((slots, GROUPS, n)),
            dma((slots, GROUPS)),
            dma((slots, GROUPS)),
        ],
        compiler_params=pltpu.CompilerParams(
            collective_id=0, has_side_effects=True, vmem_limit_bytes=60 * 2**20),
        cost_estimate=pl.CostEstimate(flops=flops, bytes_accessed=2 * channels * width,
                                      transcendentals=0),
    )(own_block, table, source_channels, channel_counts)
    weights = pair_mask[0].astype(jnp.float32) * (1.0 / math.sqrt(n))
    return (got.astype(jnp.float32) * weights[:, None, None])[None]


def solution(mesh):
    in_specs = (P("seg", "blk", None, None), P("blk", None), P("blk", None), P("blk"))
    out_specs = P("blk", None, "seg", None)
    part = functools.partial(local, mesh.shape["seg"], mesh.shape["blk"])
    return jax.shard_map(part, mesh=mesh, in_specs=in_specs, out_specs=out_specs, check_vma=False)
```

```python
import functools
import math

import ml_dtypes
import numpy as np

import jax
import jax.numpy as jnp
from jax import lax
from jax.experimental import pallas as pl
from jax.experimental.pallas import tpu as pltpu
from jax.sharding import PartitionSpec as P

LAGS = 16
REACH = 2
GROUPS = 2
PIECES = 4
AHEAD = 4
PICK = 512
MESH = pl.DeviceIdType.MESH


def make_table(bin_count, lag_count):
    lag_index = np.arange(lag_count)[:, None] - lag_count // 2
    turn_count = np.mod(np.arange(bin_count)[None, :] * lag_index, 2 * bin_count)
    phase_angle = turn_count.astype(np.float32) * np.float32(math.pi / bin_count)
    scaling = np.float32(1.0 / math.sqrt(2.0 * bin_count))
    both = np.stack([np.cos(phase_angle) * scaling, -np.sin(phase_angle) * scaling])
    return both.astype(ml_dtypes.bfloat16)


def body(n, nz, spectra_in, table_in, chosen_in, count, out, spectra, table, chosen,
         own, src, kbuf_a, kbuf_b, acc, part, landed, back, in_sem, own_send, fwd_send, src_recv,
         part_send, part_recv, back_send, back_recv):
    arrivals = [
        pltpu.make_async_copy(here, there, in_sem.at[i])
        for i, (here, there) in enumerate(
            [(chosen_in, chosen), (spectra_in, spectra), (table_in, table)])
    ]
    for arrival in arrivals:
        arrival.start()

    k = lax.axis_index("seg")
    m = lax.axis_index("blk")
    channels, width = spectra.shape
    bins = width // 2
    rows = channels // n
    group = own.shape[2]
    cols = group * LAGS
    span = bins // PIECES
    chunk = span // 2

    barrier = pltpu.get_barrier_semaphore()

    @pl.loop(1, n)
    def _(rel):
        pl.semaphore_signal(barrier, inc=1, device_id={"seg": lax.rem(k + rel, n)},
                            device_id_type=MESH)

    def along(dz):
        return jnp.logical_and(m + dz >= 0, m + dz < nz)

    for dz in (-2, -1, 1, 2):
        @pl.when(along(dz))
        def _():
            pl.semaphore_signal(barrier, inc=1, device_id={"blk": m + dz}, device_id_type=MESH)

    for arrival in arrivals:
        arrival.wait()

    channel = lax.broadcasted_iota(jnp.int32, (channels, GROUPS * group), 0)
    hit = jnp.logical_and(channel == chosen[...], channel < count[0])
    one_hot = jnp.where(hit, 1.0, 0.0).T.astype(jnp.bfloat16)

    def pick(i):
        for half in range(2):
            for c in range(0, span, PICK):
                picked = jnp.dot(one_hot, spectra[:, pl.ds(half * bins + i * span + c, PICK)],
                                 preferred_element_type=jnp.float32).astype(jnp.bfloat16)
                for g in range(GROUPS):
                    own[g, i, :, pl.ds(half * span + c, PICK)] = picked[g * group:(g + 1) * group]

    pick(0)
    live = lax.broadcasted_iota(jnp.int32, (channels, 1), 0) < count[0]
    live = jnp.where(live, 1.0, 0.0)

    near = jnp.minimum(m, REACH) + jnp.minimum(nz - 1 - m, REACH)
    pl.semaphore_wait(barrier, n - 1 + near)

    def slot_of(side, dist):
        return 1 + dist if side == 0 else 2 - dist

    def step(side):
        return 1 if side == 0 else -1

    def own_copy(side, g, i):
        return pltpu.make_async_remote_copy(
            own.at[g, i], src.at[slot_of(side, 1), g, i], own_send.at[side, g, i],
            src_recv.at[slot_of(side, 1), g, i], device_id={"blk": m + step(side)},
            device_id_type=MESH)

    def fwd_copy(side, g, i):
        return pltpu.make_async_remote_copy(
            src.at[slot_of(side, 1), g, i], src.at[slot_of(side, 2), g, i],
            fwd_send.at[side, g, i], src_recv.at[slot_of(side, 2), g, i],
            device_id={"blk": m + step(side)}, device_id_type=MESH)

    def src_wait(slot, g, i):
        here = src.at[slot, g, i]
        pltpu.make_async_copy(here, here, src_recv.at[slot, g, i]).wait()

    def part_copy(slot, g, peer, sender):
        return pltpu.make_async_remote_copy(
            part.at[slot, g, peer], landed.at[slot, g, sender], part_send.at[slot, g, peer],
            part_recv.at[slot, g, sender], device_id={"seg": peer}, device_id_type=MESH)

    def back_copy(slot, g, owner):
        at = pl.ds(pl.multiple_of(g * cols, cols), cols)
        return pltpu.make_async_remote_copy(
            back.at[slot, g], out.at[slot, :, at], back_send.at[slot, g],
            back_recv.at[slot, g], device_id={"blk": owner}, device_id_type=MESH)

    def has(side, dist):
        return m >= dist if side == 0 else m + dist < nz

    near_steps = GROUPS * PIECES
    all_steps = REACH * near_steps

    def send(t):
        g, i = lax.rem(t // PIECES, GROUPS), lax.rem(t, PIECES)
        for side in range(2):
            @pl.when(jnp.logical_and(t < near_steps, along(step(side))))
            def _():
                own_copy(side, g, i).start()

            relay = jnp.logical_and(t >= near_steps, t < all_steps)

            @pl.when(jnp.logical_and(relay, jnp.logical_and(has(side, 1), along(step(side)))))
            def _():
                fwd_copy(side, g, i).start()

    for t in range(AHEAD):
        send(jnp.int32(t))
        if t + 1 < PIECES:
            pick(t + 1)

    def expand(slot, g, i, part_of, kbuf):
        at = pl.ds(pl.multiple_of(i * span + part_of * chunk, chunk), chunk)
        t_re, t_im = table[0, :, at], table[1, :, at]
        s_re = src[slot, g, i, :, pl.ds(part_of * chunk, chunk)]
        s_im = src[slot, g, i, :, pl.ds(span + part_of * chunk, chunk)]
        for j in range(group):
            a, b = s_re[j:j + 1], s_im[j:j + 1]
            to = slice(j * LAGS, (j + 1) * LAGS)
            kbuf[to, :chunk] = a * t_re + b * t_im
            kbuf[to, chunk:] = b * t_re - a * t_im

    def contract(i, part_of, kbuf):
        dims = (((1,), (1,)), ((), ()))
        first = pl.multiple_of(i * span + part_of * chunk, chunk)
        got = lax.dot_general(kbuf[:, :chunk], spectra[:, pl.ds(first, chunk)], dims,
                              preferred_element_type=jnp.float32)
        return got + lax.dot_general(kbuf[:, chunk:], spectra[:, pl.ds(bins + first, chunk)],
                                     dims, preferred_element_type=jnp.float32)

    def correlate(side, slot, g, i):
        expand(slot, g, i, 0, kbuf_a)
        got = contract(i, 0, kbuf_a)
        expand(slot, g, i, 1, kbuf_b)
        got = got + contract(i, 1, kbuf_b)

        @pl.when(i == 0)
        def _():
            acc[side] = got

        @pl.when(i > 0)
        def _():
            acc[side] += got

    def share(side, slot, g):
        turned = acc[side].T * live
        for q in range(n):
            part[slot, g, q] = turned[q * rows:(q + 1) * rows].astype(jnp.bfloat16)

        @pl.loop(1, n)
        def _(rel):
            part_copy(slot, g, lax.rem(k + rel, n), k).start()

    def finish(p):
        dist, g = p // GROUPS + 1, p % GROUPS
        for side in range(2):
            slot = slot_of(side, dist)

            @pl.when(has(side, dist))
            def _():
                total = part[slot, g, k].astype(jnp.float32)
                for rel in range(1, n):
                    sender = lax.rem(k + rel, n)
                    part_copy(slot, g, sender, sender).wait_recv()
                    total = total + landed[slot, g, sender].astype(jnp.float32)
                back[slot, g] = total.astype(jnp.bfloat16)
                back_copy(slot, g, m - dist * step(side)).start()

    @pl.loop(0, all_steps)
    def _(t):
        p, i = t // PIECES, lax.rem(t, PIECES)
        dist, g = p // GROUPS + 1, lax.rem(p, GROUPS)
        for side in range(2):
            @pl.when(has(side, dist))
            def _():
                src_wait(slot_of(side, dist), g, i)

        send(t + AHEAD)
        for side in range(2):
            @pl.when(has(side, dist))
            def _():
                slot = slot_of(side, dist)
                correlate(side, slot, g, i)

                @pl.when(i == PIECES - 1)
                def _():
                    share(side, slot, g)

        @pl.when(jnp.logical_and(i == PIECES // 2, p > 0))
        def _():
            finish(p - 1)

    finish(REACH * GROUPS - 1)

    for slot in range(2 * REACH):
        offset = slot - REACH if slot < REACH else slot - REACH + 1

        @pl.when(jnp.logical_not(along(offset)))
        def _():
            out[slot] = jnp.zeros(out.shape[1:], out.dtype)

        @pl.when(along(offset))
        def _():
            for g in range(GROUPS):
                back_copy(slot, g, m + offset).wait_recv()

    for g in range(GROUPS):
        for side in range(2):
            @pl.when(along(step(side)))
            def _():
                for i in range(PIECES):
                    own_copy(side, g, i).wait_send()

            @pl.when(jnp.logical_and(has(side, 1), along(step(side))))
            def _():
                for i in range(PIECES):
                    fwd_copy(side, g, i).wait_send()

            for dist in range(1, REACH + 1):
                @pl.when(has(side, dist))
                def _():
                    slot = slot_of(side, dist)
                    back_copy(slot, g, m - dist * step(side)).wait_send()

                    @pl.loop(1, n)
                    def _(rel):
                        part_copy(slot, g, lax.rem(k + rel, n), k).wait_send()


def local(n, nz, spectra, source_channels, pair_mask, channel_counts):
    own_block = spectra[0, 0]
    channels, width = own_block.shape
    sources = source_channels.shape[1]
    group = sources // GROUPS
    rows, cols, slots = channels // n, group * LAGS, 2 * REACH
    table = jnp.asarray(make_table(width // 2, LAGS))
    vmem = pl.BlockSpec(memory_space=pltpu.VMEM)
    dma = pltpu.SemaphoreType.DMA
    flops = 2 * slots * channels * width * sources * LAGS
    got = pl.pallas_call(
        functools.partial(body, n, nz),
        out_shape=jax.ShapeDtypeStruct((slots, rows, sources * LAGS), jnp.bfloat16),
        in_specs=[pl.BlockSpec(memory_space=pltpu.HBM)] * 3 + [pl.BlockSpec(memory_space=pltpu.SMEM)],
        out_specs=vmem,
        scratch_shapes=[
            pltpu.VMEM(own_block.shape, jnp.bfloat16),
            pltpu.VMEM(table.shape, jnp.bfloat16),
            pltpu.VMEM((1, sources), jnp.int32),
            pltpu.VMEM((GROUPS, PIECES, group, width // PIECES), jnp.bfloat16),
            pltpu.VMEM((slots, GROUPS, PIECES, group, width // PIECES), jnp.bfloat16),
            pltpu.VMEM((cols, width // PIECES // 2), jnp.bfloat16),
            pltpu.VMEM((cols, width // PIECES // 2), jnp.bfloat16),
            pltpu.VMEM((2, cols, channels), jnp.float32),
            pltpu.VMEM((slots, GROUPS, n, rows, cols), jnp.bfloat16),
            pltpu.VMEM((slots, GROUPS, n, rows, cols), jnp.bfloat16),
            pltpu.VMEM((slots, GROUPS, rows, cols), jnp.bfloat16),
            dma((3,)),
            dma((2, GROUPS, PIECES)),
            dma((2, GROUPS, PIECES)),
            dma((slots, GROUPS, PIECES)),
            dma((slots, GROUPS, n)),
            dma((slots, GROUPS, n)),
            dma((slots, GROUPS)),
            dma((slots, GROUPS)),
        ],
        compiler_params=pltpu.CompilerParams(
            collective_id=0, has_side_effects=True, vmem_limit_bytes=40 * 2**20),
        cost_estimate=pl.CostEstimate(flops=flops, bytes_accessed=2 * channels * width,
                                      transcendentals=0),
    )(own_block, table, source_channels, channel_counts)
    weights = pair_mask[0].astype(jnp.float32) * (1.0 / math.sqrt(n))
    return (got.astype(jnp.float32) * weights[:, None, None])[None]


def solution(mesh):
    in_specs = (P("seg", "blk", None, None), P("blk", None), P("blk", None), P("blk"))
    out_specs = P("blk", None, "seg", None)
    part = functools.partial(local, mesh.shape["seg"], mesh.shape["blk"])
    return jax.shard_map(part, mesh=mesh, in_specs=in_specs, out_specs=out_specs, check_vma=False)
```

```python
import functools
import math

import ml_dtypes
import numpy as np

import jax
import jax.numpy as jnp
from jax import lax
from jax.experimental import pallas as pl
from jax.experimental.pallas import tpu as pltpu
from jax.sharding import PartitionSpec as P

LAGS = 16
REACH = 2
GROUPS = 2
PIECES = 4
AHEAD = 6
PICK = 256
MESH = pl.DeviceIdType.MESH


def make_table(bin_count, lag_count):
    lag_index = np.arange(lag_count)[:, None] - lag_count // 2
    turn_count = np.mod(np.arange(bin_count)[None, :] * lag_index, 2 * bin_count)
    phase_angle = turn_count.astype(np.float32) * np.float32(math.pi / bin_count)
    scaling = np.float32(1.0 / math.sqrt(2.0 * bin_count))
    both = np.stack([np.cos(phase_angle) * scaling, -np.sin(phase_angle) * scaling])
    return both.astype(ml_dtypes.bfloat16)


def body(n, nz, spectra_in, table_in, chosen_in, count, out, spectra, table, chosen,
         own, src, turned, wide, kbuf, acc, part, landed, back, in_sem, own_send, fwd_send, src_recv,
         part_send, part_recv, back_send, back_recv):
    arrivals = [
        pltpu.make_async_copy(here, there, in_sem.at[i])
        for i, (here, there) in enumerate(
            [(chosen_in, chosen), (spectra_in, spectra), (table_in, table)])
    ]
    for arrival in arrivals:
        arrival.start()

    k = lax.axis_index("seg")
    m = lax.axis_index("blk")
    channels, width = spectra.shape
    bins = width // 2
    rows = channels // n
    group = own.shape[2]
    cols = group * LAGS
    span = bins // PIECES
    half_cols = cols // 2

    barrier = pltpu.get_barrier_semaphore()

    @pl.loop(1, n)
    def _(rel):
        pl.semaphore_signal(barrier, inc=1, device_id={"seg": lax.rem(k + rel, n)},
                            device_id_type=MESH)

    def along(dz):
        return jnp.logical_and(m + dz >= 0, m + dz < nz)

    for dz in (-2, -1, 1, 2):
        @pl.when(along(dz))
        def _():
            pl.semaphore_signal(barrier, inc=1, device_id={"blk": m + dz}, device_id_type=MESH)

    for arrival in arrivals:
        arrival.wait()

    channel = lax.broadcasted_iota(jnp.int32, (channels, GROUPS * group), 0)
    hit = jnp.logical_and(channel == chosen[...], channel < count[0])
    one_hot = jnp.where(hit, 1.0, 0.0).T.astype(jnp.bfloat16)

    def pick(i):
        for half in range(2):
            for c in range(0, span, PICK):
                picked = jnp.dot(one_hot, spectra[:, pl.ds(half * bins + i * span + c, PICK)],
                                 preferred_element_type=jnp.float32).astype(jnp.bfloat16)
                for g in range(GROUPS):
                    own[g, i, :, pl.ds(half * span + c, PICK)] = picked[g * group:(g + 1) * group]

    pick(0)
    live = lax.broadcasted_iota(jnp.int32, (channels, 1), 0) < count[0]
    live = jnp.where(live, 1.0, 0.0)

    near = jnp.minimum(m, REACH) + jnp.minimum(nz - 1 - m, REACH)
    pl.semaphore_wait(barrier, n - 1 + near)

    def slot_of(side, dist):
        return 1 + dist if side == 0 else 2 - dist

    def step(side):
        return 1 if side == 0 else -1

    def own_copy(side, g, i):
        return pltpu.make_async_remote_copy(
            own.at[g, i], src.at[slot_of(side, 1), g, i], own_send.at[side, g, i],
            src_recv.at[slot_of(side, 1), g, i], device_id={"blk": m + step(side)},
            device_id_type=MESH)

    def fwd_copy(side, g, i):
        return pltpu.make_async_remote_copy(
            src.at[slot_of(side, 1), g, i], src.at[slot_of(side, 2), g, i],
            fwd_send.at[side, g, i], src_recv.at[slot_of(side, 2), g, i],
            device_id={"blk": m + step(side)}, device_id_type=MESH)

    def src_wait(slot, g, i):
        here = src.at[slot, g, i]
        pltpu.make_async_copy(here, here, src_recv.at[slot, g, i]).wait()

    def part_copy(slot, g, peer, sender):
        return pltpu.make_async_remote_copy(
            part.at[slot, g, peer], landed.at[slot, g, sender], part_send.at[slot, g, peer],
            part_recv.at[slot, g, sender], device_id={"seg": peer}, device_id_type=MESH)

    def back_copy(slot, g, owner):
        at = pl.ds(pl.multiple_of(g * cols, cols), cols)
        return pltpu.make_async_remote_copy(
            back.at[slot, g], out.at[slot, :, at], back_send.at[slot, g],
            back_recv.at[slot, g], device_id={"blk": owner}, device_id_type=MESH)

    def has(side, dist):
        return m >= dist if side == 0 else m + dist < nz

    near_steps = GROUPS * PIECES
    all_steps = REACH * near_steps

    def send(t):
        g, i = lax.rem(t // PIECES, GROUPS), lax.rem(t, PIECES)
        for side in range(2):
            @pl.when(jnp.logical_and(t < near_steps, along(step(side))))
            def _():
                own_copy(side, g, i).start()

            relay = jnp.logical_and(t >= near_steps, t < all_steps)

            @pl.when(jnp.logical_and(relay, jnp.logical_and(has(side, 1), along(step(side)))))
            def _():
                fwd_copy(side, g, i).start()

    for t in range(AHEAD):
        send(jnp.int32(t))
        if t + 1 < PIECES:
            pick(t + 1)

    for i in range(PIECES):
        for half in range(2):
            for c in range(0, span, PICK):
                block = spectra[:, pl.ds(half * bins + i * span + c, PICK)]
                turned[i, pl.ds(half * span + c, PICK), :] = block.T

    acc[...] = jnp.zeros_like(acc)

    def correlate(side, slot, g, i):
        wide[...] = src[slot, g, i].astype(jnp.float32)
        for h in range(2):
            for c in range(0, span, PICK):
                t_re = table[0, :, pl.ds(pl.multiple_of(i * span + c, PICK), PICK)]
                t_im = table[1, :, pl.ds(pl.multiple_of(i * span + c, PICK), PICK)]
                for j in range(group // 2):
                    row = h * (group // 2) + j
                    a = jnp.broadcast_to(wide[row:row + 1, c:c + PICK], (LAGS, PICK))
                    b = jnp.broadcast_to(wide[row:row + 1, span + c:span + c + PICK],
                                         (LAGS, PICK))
                    a, b = a.astype(jnp.bfloat16), b.astype(jnp.bfloat16)
                    to = slice(j * LAGS, (j + 1) * LAGS)
                    kbuf[h, to, c:c + PICK] = a * t_re + b * t_im
                    kbuf[h, to, span + c:span + c + PICK] = b * t_re - a * t_im
            acc[side, h * half_cols:(h + 1) * half_cols] += jnp.dot(
                kbuf[h], turned[i], preferred_element_type=jnp.float32)

    def share(side, slot, g):
        result = acc[side].T * live
        acc[side] = jnp.zeros(acc.shape[1:], acc.dtype)
        for q in range(n):
            part[slot, g, q] = result[q * rows:(q + 1) * rows].astype(jnp.bfloat16)

        @pl.loop(1, n)
        def _(rel):
            part_copy(slot, g, lax.rem(k + rel, n), k).start()

    def finish(p):
        dist, g = p // GROUPS + 1, p % GROUPS
        for side in range(2):
            slot = slot_of(side, dist)

            @pl.when(has(side, dist))
            def _():
                total = part[slot, g, k].astype(jnp.float32)
                for rel in range(1, n):
                    sender = lax.rem(k + rel, n)
                    part_copy(slot, g, sender, sender).wait_recv()
                    total = total + landed[slot, g, sender].astype(jnp.float32)
                back[slot, g] = total.astype(jnp.bfloat16)
                back_copy(slot, g, m - dist * step(side)).start()

    @pl.loop(0, all_steps)
    def _(t):
        p, i = t // PIECES, lax.rem(t, PIECES)
        dist, g = p // GROUPS + 1, lax.rem(p, GROUPS)
        for side in range(2):
            @pl.when(has(side, dist))
            def _():
                src_wait(slot_of(side, dist), g, i)

        send(t + AHEAD)
        for side in range(2):
            @pl.when(has(side, dist))
            def _():
                slot = slot_of(side, dist)
                correlate(side, slot, g, i)

                @pl.when(i == PIECES - 1)
                def _():
                    share(side, slot, g)

        @pl.when(jnp.logical_and(i == PIECES // 2, p > 0))
        def _():
            finish(p - 1)

    finish(REACH * GROUPS - 1)

    for slot in range(2 * REACH):
        offset = slot - REACH if slot < REACH else slot - REACH + 1

        @pl.when(jnp.logical_not(along(offset)))
        def _():
            out[slot] = jnp.zeros(out.shape[1:], out.dtype)

        @pl.when(along(offset))
        def _():
            for g in range(GROUPS):
                back_copy(slot, g, m + offset).wait_recv()

    for g in range(GROUPS):
        for side in range(2):
            @pl.when(along(step(side)))
            def _():
                for i in range(PIECES):
                    own_copy(side, g, i).wait_send()

            @pl.when(jnp.logical_and(has(side, 1), along(step(side))))
            def _():
                for i in range(PIECES):
                    fwd_copy(side, g, i).wait_send()

            for dist in range(1, REACH + 1):
                @pl.when(has(side, dist))
                def _():
                    slot = slot_of(side, dist)
                    back_copy(slot, g, m - dist * step(side)).wait_send()

                    @pl.loop(1, n)
                    def _(rel):
                        part_copy(slot, g, lax.rem(k + rel, n), k).wait_send()


def local(n, nz, spectra, source_channels, pair_mask, channel_counts):
    own_block = spectra[0, 0]
    channels, width = own_block.shape
    sources = source_channels.shape[1]
    group = sources // GROUPS
    rows, cols, slots = channels // n, group * LAGS, 2 * REACH
    table = jnp.asarray(make_table(width // 2, LAGS))
    vmem = pl.BlockSpec(memory_space=pltpu.VMEM)
    dma = pltpu.SemaphoreType.DMA
    flops = 2 * slots * channels * width * sources * LAGS
    got = pl.pallas_call(
        functools.partial(body, n, nz),
        out_shape=jax.ShapeDtypeStruct((slots, rows, sources * LAGS), jnp.bfloat16),
        in_specs=[pl.BlockSpec(memory_space=pl.ANY)] * 3 + [pl.BlockSpec(memory_space=pltpu.SMEM)],
        out_specs=vmem,
        scratch_shapes=[
            pltpu.VMEM(own_block.shape, jnp.bfloat16),
            pltpu.VMEM(table.shape, jnp.bfloat16),
            pltpu.VMEM((1, sources), jnp.int32),
            pltpu.VMEM((GROUPS, PIECES, group, width // PIECES), jnp.bfloat16),
            pltpu.VMEM((slots, GROUPS, PIECES, group, width // PIECES), jnp.bfloat16),
            pltpu.VMEM((PIECES, width // PIECES, channels), jnp.bfloat16),
            pltpu.VMEM((group, width // PIECES), jnp.float32),
            pltpu.VMEM((2, cols // 2, width // PIECES), jnp.bfloat16),
            pltpu.VMEM((2, cols, channels), jnp.float32),
            pltpu.VMEM((slots, GROUPS, n, rows, cols), jnp.bfloat16),
            pltpu.VMEM((slots, GROUPS, n, rows, cols), jnp.bfloat16),
            pltpu.VMEM((slots, GROUPS, rows, cols), jnp.bfloat16),
            dma((3,)),
            dma((2, GROUPS, PIECES)),
            dma((2, GROUPS, PIECES)),
            dma((slots, GROUPS, PIECES)),
            dma((slots, GROUPS, n)),
            dma((slots, GROUPS, n)),
            dma((slots, GROUPS)),
            dma((slots, GROUPS)),
        ],
        compiler_params=pltpu.CompilerParams(
            collective_id=0, has_side_effects=True, vmem_limit_bytes=60 * 2**20),
        cost_estimate=pl.CostEstimate(flops=flops, bytes_accessed=2 * channels * width,
                                      transcendentals=0),
    )(own_block, table, source_channels, channel_counts)
    weights = pair_mask[0].astype(jnp.float32) * (1.0 / math.sqrt(n))
    return (got.astype(jnp.float32) * weights[:, None, None])[None]


def solution(mesh):
    in_specs = (P("seg", "blk", None, None), P("blk", None), P("blk", None), P("blk"))
    out_specs = P("blk", None, "seg", None)
    part = functools.partial(local, mesh.shape["seg"], mesh.shape["blk"])
    return jax.shard_map(part, mesh=mesh, in_specs=in_specs, out_specs=out_specs, check_vma=False)
```

```python
import functools
import math

import ml_dtypes
import numpy as np

import jax
import jax.numpy as jnp
from jax import lax
from jax.experimental import pallas as pl
from jax.experimental.pallas import tpu as pltpu
from jax.sharding import PartitionSpec as P

LAGS = 16
REACH = 2
GROUPS = 4
PIECES = 2
AHEAD = 6
PICK = 256
MESH = pl.DeviceIdType.MESH


def make_table(bin_count, lag_count):
    lag_index = np.arange(lag_count)[:, None] - lag_count // 2
    turn_count = np.mod(np.arange(bin_count)[None, :] * lag_index, 2 * bin_count)
    phase_angle = turn_count.astype(np.float32) * np.float32(math.pi / bin_count)
    scaling = np.float32(1.0 / math.sqrt(2.0 * bin_count))
    both = np.stack([np.cos(phase_angle) * scaling, -np.sin(phase_angle) * scaling])
    return both.astype(ml_dtypes.bfloat16)


def body(n, nz, spectra_in, table_in, chosen_in, count_in, pairs_in, out, spectra, table, chosen,
         count, pairs, home,
         own, src, turned, wide, kbuf, acc, part, landed, back, in_sem, own_send, fwd_send, src_recv,
         part_send, part_recv, back_send, back_recv):
    arrivals = [
        pltpu.make_async_copy(here, there, in_sem.at[i])
        for i, (here, there) in enumerate(
            [(chosen_in, chosen), (count_in, count), (spectra_in, spectra), (pairs_in, pairs),
             (table_in, table)])
    ]
    for arrival in arrivals:
        arrival.start()

    k = lax.axis_index("seg")
    m = lax.axis_index("blk")
    channels, width = spectra.shape
    bins = width // 2
    rows = channels // n
    group = own.shape[2]
    cols = group * LAGS
    span = bins // PIECES
    half_cols = cols // 2

    barrier = pltpu.get_barrier_semaphore()

    @pl.loop(1, n)
    def _(rel):
        pl.semaphore_signal(barrier, inc=1, device_id={"seg": lax.rem(k + rel, n)},
                            device_id_type=MESH)

    def along(dz):
        return jnp.logical_and(m + dz >= 0, m + dz < nz)

    for dz in (-2, -1, 1, 2):
        @pl.when(along(dz))
        def _():
            pl.semaphore_signal(barrier, inc=1, device_id={"blk": m + dz}, device_id_type=MESH)

    for arrival in arrivals:
        arrival.wait()

    channel = lax.broadcasted_iota(jnp.int32, (channels, GROUPS * group), 0)
    hit = jnp.logical_and(channel == chosen[...], channel < count[...])
    one_hot = jnp.where(hit, 1.0, 0.0).T.astype(jnp.bfloat16)

    def pick(i):
        for half in range(2):
            for c in range(0, span, PICK):
                picked = jnp.dot(one_hot, spectra[:, pl.ds(half * bins + i * span + c, PICK)],
                                 preferred_element_type=jnp.float32).astype(jnp.bfloat16)
                for g in range(GROUPS):
                    own[g, i, :, pl.ds(half * span + c, PICK)] = picked[g * group:(g + 1) * group]

    pick(0)
    live = lax.broadcasted_iota(jnp.int32, (channels, 1), 0) < count[...]
    live = jnp.where(live, 1.0, 0.0)

    near = jnp.minimum(m, REACH) + jnp.minimum(nz - 1 - m, REACH)
    pl.semaphore_wait(barrier, n - 1 + near)

    def slot_of(side, dist):
        return 1 + dist if side == 0 else 2 - dist

    def step(side):
        return 1 if side == 0 else -1

    def own_copy(side, g, i):
        return pltpu.make_async_remote_copy(
            own.at[g, i], src.at[slot_of(side, 1), g, i], own_send.at[side, g, i],
            src_recv.at[slot_of(side, 1), g, i], device_id={"blk": m + step(side)},
            device_id_type=MESH)

    def fwd_copy(side, g, i):
        return pltpu.make_async_remote_copy(
            src.at[slot_of(side, 1), g, i], src.at[slot_of(side, 2), g, i],
            fwd_send.at[side, g, i], src_recv.at[slot_of(side, 2), g, i],
            device_id={"blk": m + step(side)}, device_id_type=MESH)

    def src_wait(slot, g, i):
        here = src.at[slot, g, i]
        pltpu.make_async_copy(here, here, src_recv.at[slot, g, i]).wait()

    def part_copy(slot, g, peer, sender):
        return pltpu.make_async_remote_copy(
            part.at[slot, g, peer], landed.at[slot, g, sender], part_send.at[slot, g, peer],
            part_recv.at[slot, g, sender], device_id={"seg": peer}, device_id_type=MESH)

    def back_copy(slot, g, owner):
        at = pl.ds(pl.multiple_of(g * cols, cols), cols)
        return pltpu.make_async_remote_copy(
            back.at[slot, g], home.at[slot, :, at], back_send.at[slot, g],
            back_recv.at[slot, g], device_id={"blk": owner}, device_id_type=MESH)

    def has(side, dist):
        return m >= dist if side == 0 else m + dist < nz

    near_steps = GROUPS * PIECES
    all_steps = REACH * near_steps

    def send(t):
        g, i = lax.rem(t // PIECES, GROUPS), lax.rem(t, PIECES)
        for side in range(2):
            @pl.when(jnp.logical_and(t < near_steps, along(step(side))))
            def _():
                own_copy(side, g, i).start()

            relay = jnp.logical_and(t >= near_steps, t < all_steps)

            @pl.when(jnp.logical_and(relay, jnp.logical_and(has(side, 1), along(step(side)))))
            def _():
                fwd_copy(side, g, i).start()

    for t in range(AHEAD):
        send(jnp.int32(t))
        if t + 1 < PIECES:
            pick(t + 1)

    for i in range(PIECES):
        for half in range(2):
            for c in range(0, span, PICK):
                block = spectra[:, pl.ds(half * bins + i * span + c, PICK)]
                turned[i, pl.ds(half * span + c, PICK), :] = block.T

    acc[...] = jnp.zeros_like(acc)

    def correlate(side, slot, g, i):
        wide[...] = src[slot, g, i].astype(jnp.float32)
        for h in range(2):
            for c in range(0, span, PICK):
                t_re = table[0, :, pl.ds(pl.multiple_of(i * span + c, PICK), PICK)]
                t_im = table[1, :, pl.ds(pl.multiple_of(i * span + c, PICK), PICK)]
                for j in range(group // 2):
                    row = h * (group // 2) + j
                    a = jnp.broadcast_to(wide[row:row + 1, c:c + PICK], (LAGS, PICK))
                    b = jnp.broadcast_to(wide[row:row + 1, span + c:span + c + PICK],
                                         (LAGS, PICK))
                    a, b = a.astype(jnp.bfloat16), b.astype(jnp.bfloat16)
                    to = slice(j * LAGS, (j + 1) * LAGS)
                    kbuf[h, to, c:c + PICK] = a * t_re + b * t_im
                    kbuf[h, to, span + c:span + c + PICK] = b * t_re - a * t_im
            acc[side, h * half_cols:(h + 1) * half_cols] += jnp.dot(
                kbuf[h], turned[i], preferred_element_type=jnp.float32)

    def share(side, slot, g):
        result = acc[side].T * live
        acc[side] = jnp.zeros(acc.shape[1:], acc.dtype)
        for q in range(n):
            part[slot, g, q] = result[q * rows:(q + 1) * rows].astype(jnp.bfloat16)

        @pl.loop(1, n)
        def _(rel):
            part_copy(slot, g, lax.rem(k + rel, n), k).start()

    def finish(p):
        dist, g = p // GROUPS + 1, p % GROUPS
        for side in range(2):
            slot = slot_of(side, dist)

            @pl.when(has(side, dist))
            def _():
                total = part[slot, g, k].astype(jnp.float32)
                for rel in range(1, n):
                    sender = lax.rem(k + rel, n)
                    part_copy(slot, g, sender, sender).wait_recv()
                    total = total + landed[slot, g, sender].astype(jnp.float32)
                back[slot, g] = total.astype(jnp.bfloat16)
                back_copy(slot, g, m - dist * step(side)).start()

    @pl.loop(0, all_steps)
    def _(t):
        p, i = t // PIECES, lax.rem(t, PIECES)
        dist, g = p // GROUPS + 1, lax.rem(p, GROUPS)
        for side in range(2):
            @pl.when(has(side, dist))
            def _():
                src_wait(slot_of(side, dist), g, i)

        send(t + AHEAD)
        for side in range(2):
            @pl.when(has(side, dist))
            def _():
                slot = slot_of(side, dist)
                correlate(side, slot, g, i)

                @pl.when(i == PIECES - 1)
                def _():
                    share(side, slot, g)

        @pl.when(jnp.logical_and(i == PIECES // 2, p > 0))
        def _():
            finish(p - 1)

    finish(REACH * GROUPS - 1)

    for slot in range(2 * REACH):
        offset = slot - REACH if slot < REACH else slot - REACH + 1

        @pl.when(jnp.logical_not(along(offset)))
        def _():
            out[slot] = jnp.zeros(out.shape[1:], out.dtype)

        @pl.when(along(offset))
        def _():
            for g in range(GROUPS):
                back_copy(slot, g, m + offset).wait_recv()
            weight = pairs[:, slot:slot + 1].astype(jnp.float32) * (1.0 / math.sqrt(n))
            out[slot] = home[slot].astype(jnp.float32) * weight

    for g in range(GROUPS):
        for side in range(2):
            @pl.when(along(step(side)))
            def _():
                for i in range(PIECES):
                    own_copy(side, g, i).wait_send()

            @pl.when(jnp.logical_and(has(side, 1), along(step(side))))
            def _():
                for i in range(PIECES):
                    fwd_copy(side, g, i).wait_send()

            for dist in range(1, REACH + 1):
                @pl.when(has(side, dist))
                def _():
                    slot = slot_of(side, dist)
                    back_copy(slot, g, m - dist * step(side)).wait_send()

                    @pl.loop(1, n)
                    def _(rel):
                        part_copy(slot, g, lax.rem(k + rel, n), k).wait_send()


def local(n, nz, spectra, source_channels, pair_mask, channel_counts):
    own_block = spectra[0, 0]
    channels, width = own_block.shape
    sources = source_channels.shape[1]
    group = sources // GROUPS
    rows, cols, slots = channels // n, group * LAGS, 2 * REACH
    table = jnp.asarray(make_table(width // 2, LAGS))
    vmem = pl.BlockSpec(memory_space=pltpu.VMEM)
    dma = pltpu.SemaphoreType.DMA
    flops = 2 * slots * channels * width * sources * LAGS
    got = pl.pallas_call(
        functools.partial(body, n, nz),
        out_shape=jax.ShapeDtypeStruct((slots, rows, sources * LAGS), jnp.float32),
        in_specs=[pl.BlockSpec(memory_space=pl.ANY)] * 5,
        out_specs=vmem,
        scratch_shapes=[
            pltpu.VMEM(own_block.shape, jnp.bfloat16),
            pltpu.VMEM(table.shape, jnp.bfloat16),
            pltpu.VMEM((1, sources), jnp.int32),
            pltpu.VMEM((1, 1), jnp.int32),
            pltpu.VMEM((1, slots), jnp.int32),
            pltpu.VMEM((slots, rows, sources * LAGS), jnp.bfloat16),
            pltpu.VMEM((GROUPS, PIECES, group, width // PIECES), jnp.bfloat16),
            pltpu.VMEM((slots, GROUPS, PIECES, group, width // PIECES), jnp.bfloat16),
            pltpu.VMEM((PIECES, width // PIECES, channels), jnp.bfloat16),
            pltpu.VMEM((group, width // PIECES), jnp.float32),
            pltpu.VMEM((2, cols // 2, width // PIECES), jnp.bfloat16),
            pltpu.VMEM((2, cols, channels), jnp.float32),
            pltpu.VMEM((slots, GROUPS, n, rows, cols), jnp.bfloat16),
            pltpu.VMEM((slots, GROUPS, n, rows, cols), jnp.bfloat16),
            pltpu.VMEM((slots, GROUPS, rows, cols), jnp.bfloat16),
            dma((5,)),
            dma((2, GROUPS, PIECES)),
            dma((2, GROUPS, PIECES)),
            dma((slots, GROUPS, PIECES)),
            dma((slots, GROUPS, n)),
            dma((slots, GROUPS, n)),
            dma((slots, GROUPS)),
            dma((slots, GROUPS)),
        ],
        compiler_params=pltpu.CompilerParams(
            collective_id=0, has_side_effects=True, vmem_limit_bytes=60 * 2**20),
        cost_estimate=pl.CostEstimate(flops=flops, bytes_accessed=2 * channels * width,
                                      transcendentals=0),
    )(own_block, table, source_channels, channel_counts.reshape(1, 1), pair_mask)
    return got[None]


def solution(mesh):
    in_specs = (P("seg", "blk", None, None), P("blk", None), P("blk", None), P("blk"))
    out_specs = P("blk", None, "seg", None)
    part = functools.partial(local, mesh.shape["seg"], mesh.shape["blk"])
    return jax.shard_map(part, mesh=mesh, in_specs=in_specs, out_specs=out_specs, check_vma=False)
```

```python
import functools
import math

import ml_dtypes
import numpy as np

import jax
import jax.numpy as jnp
from jax import lax
from jax.experimental import pallas as pl
from jax.experimental.pallas import tpu as pltpu
from jax.sharding import PartitionSpec as P

LAGS = 16
REACH = 2
GROUPS = 2
PIECES = 4
PICK = 512
MESH = pl.DeviceIdType.MESH


def make_table(bin_count, lag_count):
    lag_index = np.arange(lag_count)[:, None] - lag_count // 2
    turn_count = np.mod(np.arange(bin_count)[None, :] * lag_index, 2 * bin_count)
    phase_angle = turn_count.astype(np.float32) * np.float32(math.pi / bin_count)
    scaling = np.float32(1.0 / math.sqrt(2.0 * bin_count))
    both = np.stack([np.cos(phase_angle) * scaling, -np.sin(phase_angle) * scaling])
    return both.astype(ml_dtypes.bfloat16)


def body(n, nz, spectra_in, table_in, chosen_in, count_in, out, spectra, table, chosen, count,
         own, src, kbuf_a, kbuf_b, acc, part, landed, back, in_sem, own_send, fwd_send, src_recv,
         part_send, part_recv, back_send, back_recv):
    arrivals = [
        pltpu.make_async_copy(here, there, in_sem.at[i])
        for i, (here, there) in enumerate([(chosen_in, chosen), (count_in, count),
                                           (spectra_in, spectra), (table_in, table)])
    ]
    for arrival in arrivals:
        arrival.start()

    k = lax.axis_index("seg")
    m = lax.axis_index("blk")
    channels, width = spectra.shape
    bins = width // 2
    rows = channels // n
    group = own.shape[2]
    cols = group * LAGS
    span = bins // PIECES
    chunk = span // 2

    barrier = pltpu.get_barrier_semaphore()

    @pl.loop(1, n)
    def _(rel):
        pl.semaphore_signal(barrier, inc=1, device_id={"seg": lax.rem(k + rel, n)},
                            device_id_type=MESH)

    def along(dz):
        return jnp.logical_and(m + dz >= 0, m + dz < nz)

    for dz in (-2, -1, 1, 2):
        @pl.when(along(dz))
        def _():
            pl.semaphore_signal(barrier, inc=1, device_id={"blk": m + dz}, device_id_type=MESH)

    for arrival in arrivals:
        arrival.wait()

    channel = lax.broadcasted_iota(jnp.int32, (channels, GROUPS * group), 0)
    hit = jnp.logical_and(channel == chosen[...], channel < count[0])
    one_hot = jnp.where(hit, 1.0, 0.0).T.astype(jnp.bfloat16)
    for i in range(PIECES):
        for half in range(2):
            for c in range(0, span, PICK):
                picked = jnp.dot(one_hot, spectra[:, pl.ds(half * bins + i * span + c, PICK)],
                                 preferred_element_type=jnp.float32).astype(jnp.bfloat16)
                for g in range(GROUPS):
                    own[g, i, :, pl.ds(half * span + c, PICK)] = picked[g * group:(g + 1) * group]
    live = lax.broadcasted_iota(jnp.int32, (channels, 1), 0) < count[0]
    live = jnp.where(live, 1.0, 0.0)

    near = jnp.minimum(m, REACH) + jnp.minimum(nz - 1 - m, REACH)
    pl.semaphore_wait(barrier, n - 1 + near)

    def slot_of(side, dist):
        return 1 + dist if side == 0 else 2 - dist

    def step(side):
        return 1 if side == 0 else -1

    def own_copy(side, g, i):
        return pltpu.make_async_remote_copy(
            own.at[g, i], src.at[slot_of(side, 1), g, i], own_send.at[side, g, i],
            src_recv.at[slot_of(side, 1), g, i], device_id={"blk": m + step(side)},
            device_id_type=MESH)

    def fwd_copy(side, g, i):
        return pltpu.make_async_remote_copy(
            src.at[slot_of(side, 1), g, i], src.at[slot_of(side, 2), g, i],
            fwd_send.at[side, g, i], src_recv.at[slot_of(side, 2), g, i],
            device_id={"blk": m + step(side)}, device_id_type=MESH)

    def src_wait(slot, g, i):
        here = src.at[slot, g, i]
        pltpu.make_async_copy(here, here, src_recv.at[slot, g, i]).wait()

    def part_copy(slot, g, peer, sender):
        return pltpu.make_async_remote_copy(
            part.at[slot, g, peer], landed.at[slot, g, sender], part_send.at[slot, g, peer],
            part_recv.at[slot, g, sender], device_id={"seg": peer}, device_id_type=MESH)

    def back_copy(slot, g, owner):
        at = pl.ds(pl.multiple_of(g * cols, cols), cols)
        return pltpu.make_async_remote_copy(
            back.at[slot, g], out.at[slot, :, at], back_send.at[slot, g],
            back_recv.at[slot, g], device_id={"blk": owner}, device_id_type=MESH)

    def has(side, dist):
        return m >= dist if side == 0 else m + dist < nz

    for g in range(GROUPS):
        for side in range(2):
            @pl.when(along(step(side)))
            def _():
                for i in range(PIECES):
                    own_copy(side, g, i).start()

    def expand(slot, g, i, part_of, kbuf):
        at = pl.ds(pl.multiple_of(i * span + part_of * chunk, chunk), chunk)
        t_re, t_im = table[0, :, at], table[1, :, at]
        s_re = src[slot, g, i, :, pl.ds(part_of * chunk, chunk)]
        s_im = src[slot, g, i, :, pl.ds(span + part_of * chunk, chunk)]
        for j in range(group):
            a, b = s_re[j:j + 1], s_im[j:j + 1]
            to = slice(j * LAGS, (j + 1) * LAGS)
            kbuf[to, :chunk] = a * t_re + b * t_im
            kbuf[to, chunk:] = b * t_re - a * t_im

    def contract(i, part_of, kbuf):
        dims = (((1,), (1,)), ((), ()))
        first = pl.multiple_of(i * span + part_of * chunk, chunk)
        got = lax.dot_general(kbuf[:, :chunk], spectra[:, pl.ds(first, chunk)], dims,
                              preferred_element_type=jnp.float32)
        return got + lax.dot_general(kbuf[:, chunk:], spectra[:, pl.ds(bins + first, chunk)],
                                     dims, preferred_element_type=jnp.float32)

    def correlate(slot, dist, g):
        acc[...] = jnp.zeros_like(acc)

        @pl.loop(0, PIECES)
        def _(i):
            @pl.when(dist > 1)
            def _():
                src_wait(slot, g, i)

            expand(slot, g, i, 0, kbuf_a)
            got = contract(i, 0, kbuf_a)
            expand(slot, g, i, 1, kbuf_b)
            acc[...] += got + contract(i, 1, kbuf_b)

        turned = acc[...].T * live
        for q in range(n):
            part[slot, g, q] = turned[q * rows:(q + 1) * rows].astype(jnp.bfloat16)

        @pl.loop(1, n)
        def _(rel):
            part_copy(slot, g, lax.rem(k + rel, n), k).start()

    def finish(p):
        dist, g = p // GROUPS + 1, p % GROUPS
        for side in range(2):
            slot = slot_of(side, dist)

            @pl.when(has(side, dist))
            def _():
                total = part[slot, g, k].astype(jnp.float32)
                for rel in range(1, n):
                    sender = lax.rem(k + rel, n)
                    part_copy(slot, g, sender, sender).wait_recv()
                    total = total + landed[slot, g, sender].astype(jnp.float32)
                back[slot, g] = total.astype(jnp.bfloat16)
                back_copy(slot, g, m - dist * step(side)).start()

    @pl.loop(0, REACH * GROUPS)
    def _(p):
        dist, g = p // GROUPS + 1, p % GROUPS
        for side in range(2):
            for i in range(PIECES):
                @pl.when(jnp.logical_and(dist == 1, has(side, 1)))
                def _():
                    src_wait(slot_of(side, 1), g, i)

                    @pl.when(along(step(side)))
                    def _():
                        fwd_copy(side, g, i).start()

        for side in range(2):
            @pl.when(has(side, dist))
            def _():
                correlate(slot_of(side, dist), dist, g)

        @pl.when(p > 0)
        def _():
            finish(p - 1)

    finish(REACH * GROUPS - 1)

    for slot in range(2 * REACH):
        offset = slot - REACH if slot < REACH else slot - REACH + 1

        @pl.when(jnp.logical_not(along(offset)))
        def _():
            out[slot] = jnp.zeros(out.shape[1:], out.dtype)

        @pl.when(along(offset))
        def _():
            for g in range(GROUPS):
                back_copy(slot, g, m + offset).wait_recv()

    for g in range(GROUPS):
        for side in range(2):
            @pl.when(along(step(side)))
            def _():
                for i in range(PIECES):
                    own_copy(side, g, i).wait_send()

            @pl.when(jnp.logical_and(has(side, 1), along(step(side))))
            def _():
                for i in range(PIECES):
                    fwd_copy(side, g, i).wait_send()

            for dist in range(1, REACH + 1):
                @pl.when(has(side, dist))
                def _():
                    slot = slot_of(side, dist)
                    back_copy(slot, g, m - dist * step(side)).wait_send()

                    @pl.loop(1, n)
                    def _(rel):
                        part_copy(slot, g, lax.rem(k + rel, n), k).wait_send()


def local(n, nz, spectra, source_channels, pair_mask, channel_counts):
    own_block = spectra[0, 0]
    channels, width = own_block.shape
    sources = source_channels.shape[1]
    group = sources // GROUPS
    rows, cols, slots = channels // n, group * LAGS, 2 * REACH
    table = jnp.asarray(make_table(width // 2, LAGS))
    vmem = pl.BlockSpec(memory_space=pltpu.VMEM)
    dma = pltpu.SemaphoreType.DMA
    flops = 2 * slots * channels * width * sources * LAGS
    got = pl.pallas_call(
        functools.partial(body, n, nz),
        out_shape=jax.ShapeDtypeStruct((slots, rows, sources * LAGS), jnp.bfloat16),
        in_specs=[pl.BlockSpec(memory_space=pl.ANY)] * 4,
        out_specs=vmem,
        scratch_shapes=[
            pltpu.VMEM(own_block.shape, jnp.bfloat16),
            pltpu.VMEM(table.shape, jnp.bfloat16),
            pltpu.VMEM((1, sources), jnp.int32),
            pltpu.SMEM((1,), jnp.int32),
            pltpu.VMEM((GROUPS, PIECES, group, width // PIECES), jnp.bfloat16),
            pltpu.VMEM((slots, GROUPS, PIECES, group, width // PIECES), jnp.bfloat16),
            pltpu.VMEM((cols, width // PIECES // 2), jnp.bfloat16),
            pltpu.VMEM((cols, width // PIECES // 2), jnp.bfloat16),
            pltpu.VMEM((cols, channels), jnp.float32),
            pltpu.VMEM((slots, GROUPS, n, rows, cols), jnp.bfloat16),
            pltpu.VMEM((slots, GROUPS, n, rows, cols), jnp.bfloat16),
            pltpu.VMEM((slots, GROUPS, rows, cols), jnp.bfloat16),
            dma((4,)),
            dma((2, GROUPS, PIECES)),
            dma((2, GROUPS, PIECES)),
            dma((slots, GROUPS, PIECES)),
            dma((slots, GROUPS, n)),
            dma((slots, GROUPS, n)),
            dma((slots, GROUPS)),
            dma((slots, GROUPS)),
        ],
        compiler_params=pltpu.CompilerParams(
            collective_id=0, has_side_effects=True, vmem_limit_bytes=53 * 2**20),
        cost_estimate=pl.CostEstimate(flops=flops, bytes_accessed=2 * channels * width,
                                      transcendentals=0),
    )(own_block, table, source_channels, channel_counts)
    weights = pair_mask[0].astype(jnp.float32) * (1.0 / math.sqrt(n))
    return (got.astype(jnp.float32) * weights[:, None, None])[None]


def solution(mesh):
    in_specs = (P("seg", "blk", None, None), P("blk", None), P("blk", None), P("blk"))
    out_specs = P("blk", None, "seg", None)
    part = functools.partial(local, mesh.shape["seg"], mesh.shape["blk"])
    return jax.shard_map(part, mesh=mesh, in_specs=in_specs, out_specs=out_specs, check_vma=False)
```
